32 devices in a mesh: seg: 2 (over core), dp: 16 (over z, y, x).
Axes of the slice: x: 2, y: 2, z: 4, core: 2. Of those that a mesh axis runs over, the one named last changes fastest.
Arguments:
- query_rows: bfloat16 [16, 1024, 1280], P('dp', 'seg'), may hold values from -160 to 160
- key_rows: bfloat16 [16, 1024, 1280], P('dp', 'seg'), may hold values from -8 to 8
- value_rows: bfloat16 [16, 1024, 1280], P('dp', 'seg'), may hold values from -6 to 6
- prompt_keys: bfloat16 [16, 100, 1280], P('dp', 'seg'), may hold values from -6 to 6
- prompt_values: bfloat16 [16, 100, 1280], P('dp', 'seg'), may hold values from -6 to 6
- out_grad: bfloat16 [16, 1024, 2560], P('dp', 'seg'), may hold values from -54 to 54
- w_out: bfloat16 [1280, 2560], replicated, may hold values from -0.15625 to 0.15625
Outputs:
- query_grad: bfloat16 [16, 1024, 1280], P('dp', 'seg')
- key_grad: bfloat16 [16, 1024, 1280], P('dp', 'seg')
- value_grad: bfloat16 [16, 1024, 1280], P('dp', 'seg')
- prompt_key_grad: bfloat16 [16, 100, 1280], P('dp', 'seg')
- prompt_value_grad: bfloat16 [16, 100, 1280], P('dp', 'seg')
- weight_grad: bfloat16 [1280, 2560], replicated
The draws below stay inside these ranges and needn't reach their ends.
All inputs are finite; a program needn't handle non-finite values.
Results may differ from the reference program's by a relative error of at most 0.0058.
Values may be sent and summed in bfloat16 or wider, within the bound.
A program may use at most 256 MiB of HBM per device.

```python
import jax
import jax.numpy as jnp
from jax import lax

D = 2560
HEADS = 16
HD = 80
SUMS = 50
TOK = 512
SEQ = 1024
DOCS = 16
N_SEG = 2


def pair_rows(key):
    shape = (DOCS, SEQ, HEADS * HD)
    base_keys = jnp.clip(jax.random.normal(jax.random.fold_in(key, 11), shape, jnp.float32), -6.0, 6.0)
    base_query = jnp.clip(jax.random.normal(jax.random.fold_in(key, 12), shape, jnp.float32), -6.0, 6.0)
    return (base_query, base_keys)


def draw_query_rows(key, part):
    return pair_rows(key)[0].astype(jnp.bfloat16)


def draw_key_rows(key, part):
    return pair_rows(key)[1].astype(jnp.bfloat16)


def draw_out_grad(key, part):
    base = jnp.clip(jax.random.normal(jax.random.fold_in(key, 21), (DOCS, SEQ, D), jnp.float32), -6.0, 6.0)
    rising = 1.0 + 2.0 * jnp.arange(SEQ, dtype=jnp.float32) / SEQ
    by_doc = 1.0 + 2.0 * jnp.arange(DOCS, dtype=jnp.float32) / DOCS
    return (base * rising[None, :, None] * by_doc[:, None, None]).astype(jnp.bfloat16)


def levels(rng, dims, pieces, least, top_value):
    loudness = 1.0
    for dim, parts in pieces:
        heights = jax.random.uniform(jax.random.fold_in(jax.random.fold_in(rng, 6), dim), (parts,), jnp.float32, least / len(pieces), top_value / len(pieces))
        loudness = loudness * jnp.repeat(jnp.exp(heights), dims[dim] // parts).reshape((-1,) + (1,) * (len(dims) - 1 - dim))
    return loudness


def bell_draw(key, extent, scale, limit, pieces=(), kind=jnp.bfloat16):
    result = scale * jax.random.normal(key, extent, jnp.float32)
    if pieces:
        result = result * levels(key, extent, pieces, -0.22, 0.18)
    return jnp.clip(result, -limit, limit).astype(kind)


def setup_inputs(seed: int = 0) -> dict:
    seeds = jax.random.split(jax.random.key(seed), 8)
    return {
        "query_rows": draw_query_rows(jax.random.fold_in(seeds[7], 71), 0),
        "key_rows": draw_key_rows(jax.random.fold_in(seeds[7], 71), 0),
        "value_rows": bell_draw(seeds[2], (DOCS, SEQ, HEADS * HD), 1.0, 6.0, ((0, 16), (1, 2))),
        "prompt_keys": bell_draw(seeds[3], (DOCS, N_SEG * SUMS, HEADS * HD), 1.0, 6.0, ((0, 16), (1, 2))),
        "prompt_values": bell_draw(seeds[4], (DOCS, N_SEG * SUMS, HEADS * HD), 1.0, 6.0, ((0, 16), (1, 2))),
        "out_grad": draw_out_grad(jax.random.fold_in(seeds[7], 71), 0),
        "w_out": bell_draw(seeds[6], (HEADS * HD, D), (HEADS * HD) ** -0.5, 0.15625),
    }


def attend_back(query_seg, key_seg, value_seg, prompt_k, prompt_v, head_low, segment):
    tokens_dev = query_seg.shape[0]
    head_size = query_seg.shape[1] // HEADS
    scaling = head_size ** (-0.5)
    prefix = prompt_k.shape[0]
    keys_all = jnp.concatenate([prompt_k, key_seg], 0).astype(jnp.float32).reshape(-1, HEADS, head_size)
    values_all = jnp.concatenate([prompt_v, value_seg], 0).astype(jnp.float32).reshape(-1, HEADS, head_size)
    query_heads = query_seg.astype(jnp.float32).reshape(tokens_dev, HEADS, head_size)
    grad_heads = head_low.astype(jnp.float32).reshape(tokens_dev, HEADS, head_size)
    scores = jnp.einsum('qhd,khd->hqk', query_heads, keys_all) * scaling
    row_ids = jnp.arange(tokens_dev, dtype=jnp.int32)
    col_ids = jnp.arange(prefix + tokens_dev, dtype=jnp.int32)
    visible = jnp.where(col_ids[None, :] < prefix, (col_ids // SUMS < segment)[None, :], (col_ids - prefix)[None, :] <= row_ids[:, None])
    scores = jnp.where(visible[None], scores, jnp.float32(-1e+30))
    row_max = lax.optimization_barrier(jnp.max(scores, -1, keepdims=True))
    weights = jnp.exp(scores - row_max)
    probs = weights / lax.optimization_barrier(jnp.sum(weights, -1, keepdims=True))
    probs_low = probs.astype(jnp.bfloat16).astype(jnp.float32)
    attn = jnp.einsum('hqk,khd->qhd', probs_low, values_all).reshape(tokens_dev, -1).astype(jnp.bfloat16)
    prob_grad = jnp.einsum('qhd,khd->hqk', grad_heads, values_all)
    row_delta = lax.optimization_barrier(jnp.sum(probs * prob_grad, -1, keepdims=True))
    score_grad = (scaling * probs * (prob_grad - row_delta)).astype(jnp.bfloat16).astype(jnp.float32)
    query_grad = jnp.einsum('hqk,khd->qhd', score_grad, keys_all).reshape(tokens_dev, -1).astype(jnp.bfloat16)
    key_all_grad = jnp.einsum('hqk,qhd->khd', score_grad, query_heads).reshape(prefix + tokens_dev, -1)
    value_all_grad = jnp.einsum('hqk,qhd->khd', probs_low, grad_heads).reshape(prefix + tokens_dev, -1)
    return (query_grad, key_all_grad[prefix:].astype(jnp.bfloat16), value_all_grad[prefix:].astype(jnp.bfloat16), key_all_grad[:prefix], value_all_grad[:prefix], attn)

def reference(query_rows, key_rows, value_rows, prompt_keys, prompt_values, out_grad, w_out):
    width = query_rows.shape[2]
    head_grad = jnp.dot(out_grad.reshape(-1, D), w_out.T, preferred_element_type=jnp.float32)
    head_grad = head_grad.astype(jnp.bfloat16).reshape(DOCS, SEQ, width)

    def visit(carry, position):
        weight_acc, pk_acc, pv_acc = carry
        doc = position // N_SEG
        segment = position % N_SEG
        start = (segment * TOK).astype(jnp.int32)

        def take(array):
            return lax.dynamic_slice_in_dim(array[doc], start, TOK, 0)
        outputs = attend_back(take(query_rows), take(key_rows), take(value_rows), prompt_keys[doc], prompt_values[doc], take(head_grad), segment)
        query_grad, key_grad, value_grad, pk_part, pv_part, attn = outputs
        weight_acc = weight_acc + jnp.dot(attn.T, take(out_grad), preferred_element_type=jnp.float32)
        pk_acc = pk_acc.at[doc].add(pk_part)
        pv_acc = pv_acc.at[doc].add(pv_part)
        return ((weight_acc, pk_acc, pv_acc), (query_grad, key_grad, value_grad))
    start_carry = (jnp.zeros((width, D), jnp.float32), jnp.zeros((DOCS, N_SEG * SUMS, width), jnp.float32), jnp.zeros((DOCS, N_SEG * SUMS, width), jnp.float32))
    positions = jnp.arange(DOCS * N_SEG, dtype=jnp.int32)
    final, stacked = lax.scan(visit, start_carry, positions)
    weight_acc, pk_acc, pv_acc = final
    rms_value = jnp.sqrt(jnp.mean(weight_acc * weight_acc) + 1e-06)
    weight_grad = (weight_acc * jnp.minimum(1.0, 1.0 / rms_value)).astype(jnp.bfloat16)
    query_grad = stacked[0].reshape(DOCS, SEQ, width)
    key_grad = stacked[1].reshape(DOCS, SEQ, width)
    value_grad = stacked[2].reshape(DOCS, SEQ, width)
    return (query_grad, key_grad, value_grad, pk_acc.astype(jnp.bfloat16), pv_acc.astype(jnp.bfloat16), weight_grad)
```

```python
import functools

import jax
import jax.numpy as jnp
from jax import lax
from jax.experimental import pallas as pl
from jax.experimental.pallas import tpu as pltpu
from jax.sharding import PartitionSpec as P

HEADS = 16
GROUP = 8
BLOCK = 16
LOG2E = 1.4426950408889634


def dot(a, b, contract):
    return lax.dot_general(a, b, (contract, ((), ())), preferred_element_type=jnp.float32)


def hidden(pad, prefix_visible, keys, first_query, queries):
    rows = lax.broadcasted_iota(jnp.int32, (keys, queries), 0)
    cols = lax.broadcasted_iota(jnp.int32, (keys, queries), 1) + first_query
    return jnp.where(rows < pad, rows + 1 - prefix_visible, rows - pad - cols) > 0


def spans(tokens):
    size = tokens // 2 if tokens % 256 == 0 else tokens
    return [(start, size) for start in range(0, tokens, size)]


def fwd_kernel(sums, head_size, q_ref, k_ref, v_ref, pk_ref, pv_ref, attn_ref, max_ref, inv_ref):
    tokens, pad = q_ref.shape[0], pk_ref.shape[0]
    visible = lax.axis_index("seg") * sums
    scale = head_size**-0.5 * LOG2E
    for start, size in spans(tokens):
        own = start + size
        mask = hidden(pad, visible, pad + own, start, size)
        for head in range(q_ref.shape[1] // head_size):
            lanes = slice(head * head_size, (head + 1) * head_size)
            keys = jnp.concatenate([pk_ref[:, lanes], k_ref[:own, lanes]], 0)
            values = jnp.concatenate([pv_ref[:, lanes], v_ref[:own, lanes]], 0)
            scores = dot(keys, q_ref[start:own, lanes], ((1,), (1,)))
            scores = jnp.where(mask, jnp.float32(-1e30), scores)
            top = jnp.max(scores, 0, keepdims=True)
            weights = jnp.exp2((scores - top) * scale)
            inverse = 1.0 / jnp.sum(weights, 0, keepdims=True)
            probs_low = (weights * inverse).astype(jnp.bfloat16)
            attn = dot(values, probs_low, ((0,), (0,)))
            attn_ref[lanes, start:own] = attn.astype(jnp.bfloat16)
            max_ref[head : head + 1, start:own] = top
            inv_ref[head : head + 1, start:own] = inverse


def bwd_kernel(
    sums,
    head_size,
    q_ref,
    k_ref,
    v_ref,
    pk_ref,
    pv_ref,
    g_ref,
    max_ref,
    inv_ref,
    dq_ref,
    dk_ref,
    dv_ref,
    dpk_ref,
    dpv_ref,
    dq_t,
):
    tokens, pad = q_ref.shape[0], pk_ref.shape[0]
    visible = lax.axis_index("seg") * sums
    scaling = head_size**-0.5
    parts = spans(tokens)
    masks = [hidden(pad, visible, pad + start + size, start, size) for start, size in parts]
    for head in range(q_ref.shape[1] // head_size):
        lanes = slice(head * head_size, (head + 1) * head_size)
        key_sum, value_sum = [], []
        for (start, size), mask in zip(parts, masks):
            own = start + size
            keys = jnp.concatenate([pk_ref[:, lanes], k_ref[:own, lanes]], 0)
            values = jnp.concatenate([pv_ref[:, lanes], v_ref[:own, lanes]], 0)
            query, grad = q_ref[start:own, lanes], g_ref[start:own, lanes]
            scores = dot(keys, query, ((1,), (1,)))
            scores = jnp.where(mask, jnp.float32(-1e30), scores)
            top = max_ref[head : head + 1, start:own]
            inverse = inv_ref[head : head + 1, start:own]
            probs = jnp.exp2((scores - top) * (scaling * LOG2E)) * inverse
            prob_grad = dot(values, grad, ((1,), (1,)))
            weighted = probs * prob_grad
            row_delta = jnp.sum(weighted, 0, keepdims=True)
            score_grad = (scaling * (weighted - probs * row_delta)).astype(jnp.bfloat16)
            probs_low = probs.astype(jnp.bfloat16)
            dq_t[lanes, start:own] = dot(keys, score_grad, ((0,), (0,)))
            key_sum.append(dot(score_grad, query, ((1,), (0,))))
            value_sum.append(dot(probs_low, grad, ((1,), (0,))))
        for sum_list, own_ref, prompt_ref in (
            (key_sum, dk_ref, dpk_ref),
            (value_sum, dv_ref, dpv_ref),
        ):
            total = sum_list[-1]
            for part in sum_list[:-1]:
                count = part.shape[0]
                total = jnp.concatenate([total[:count] + part, total[count:]], 0)
            prompt_ref[:, lanes] = total[:pad].astype(jnp.bfloat16)
            own_ref[:, lanes] = total[pad:].astype(jnp.bfloat16)
    dq_ref[...] = dq_t[...].T.astype(jnp.bfloat16)


def lanes_block(rows, width):
    return pl.BlockSpec((rows, width), lambda g: (0, g))


def rows_block(rows, width):
    return pl.BlockSpec((rows, width), lambda g: (g, 0))


def shards(n_seg, n_dp, query, key, value, prompt_keys, prompt_values, out_grad, w_out):
    query, key, value, out_grad = query[0], key[0], value[0], out_grad[0]
    tokens, width = query.shape
    sums = prompt_keys.shape[1]
    head_size = width // HEADS
    group = GROUP * head_size
    read = (n_seg - 1) * sums
    pad = -(-read // 64) * 64
    prompts = jnp.stack([prompt_keys[0], prompt_values[0]])
    prompts = lax.all_gather(prompts, "seg", axis=1, tiled=True)[:, :read]
    prompts = jnp.pad(prompts, ((0, 0), (0, pad - read), (0, 0)))
    prompt_k, prompt_v = prompts[0], prompts[1]
    params = pltpu.CompilerParams(vmem_limit_bytes=48 * 1024 * 1024)
    own_spec, prompt_spec = lanes_block(tokens, group), lanes_block(pad, group)
    stat_spec = rows_block(GROUP, tokens)
    stat = jax.ShapeDtypeStruct((HEADS, tokens), jnp.float32)
    low = functools.partial(jax.ShapeDtypeStruct, dtype=jnp.bfloat16)
    flops = 2 * HEADS * tokens * tokens * head_size

    attn_t, top, inverse = pl.pallas_call(
        functools.partial(fwd_kernel, sums, head_size),
        grid=(HEADS // GROUP,),
        in_specs=[own_spec] * 3 + [prompt_spec] * 2,
        out_specs=[rows_block(group, tokens), stat_spec, stat_spec],
        out_shape=[low((width, tokens)), stat, stat],
        compiler_params=params,
        cost_estimate=pl.CostEstimate(
            flops=10 * flops, bytes_accessed=8 * tokens * width, transcendentals=0
        ),
    )(query, key, value, prompt_k, prompt_v)

    plan = split_plan(n_seg, n_dp, width, out_grad.shape[1])
    if plan is None:
        weight_grad = plain_weight(attn_t, out_grad)
    else:
        weight_grad = sum_weight(n_seg, n_dp, plan, attn_t, out_grad)

    head_low = jnp.einsum("td,hd->th", out_grad, w_out, preferred_element_type=jnp.float32)
    query_grad, key_grad, value_grad, pk_part, pv_part = pl.pallas_call(
        functools.partial(bwd_kernel, sums, head_size),
        grid=(HEADS // GROUP,),
        in_specs=[own_spec] * 3 + [prompt_spec] * 2 + [own_spec, stat_spec, stat_spec],
        out_specs=[own_spec] * 3 + [prompt_spec] * 2,
        out_shape=[low((tokens, width))] * 3 + [low((pad, width))] * 2,
        scratch_shapes=[pltpu.VMEM((group, tokens), jnp.float32)],
        compiler_params=params,
        cost_estimate=pl.CostEstimate(
            flops=25 * flops, bytes_accessed=16 * tokens * width, transcendentals=0
        ),
    )(query, key, value, prompt_k, prompt_v, head_low.astype(jnp.bfloat16), top, inverse)

    parts = jnp.stack([pk_part, pv_part])
    segment = lax.axis_index("seg")
    later = jnp.zeros((2, sums, width), jnp.float32)
    for step in range(1, n_seg):
        start = jnp.maximum(segment - step, 0) * sums
        block = lax.dynamic_slice_in_dim(parts, start, sums, 1)
        pairs = [(at, at - step) for at in range(step, n_seg)]
        later = later + lax.ppermute(block, "seg", pairs).astype(jnp.float32)
    later = later.astype(jnp.bfloat16)

    return (
        query_grad[None],
        key_grad[None],
        value_grad[None],
        later[0][None],
        later[1][None],
        weight_grad,
    )


def plain_weight(attn_t, out_grad):
    part = jnp.dot(attn_t, out_grad, preferred_element_type=jnp.float32)
    total = lax.psum(part, ("seg", "dp"))
    rms = jnp.sqrt(jnp.mean(total * total) + 1e-06)
    return (total * jnp.minimum(1.0, 1.0 / rms)).astype(jnp.bfloat16)


def split_plan(n_seg, n_dp, rows, cols):
    bits = n_dp.bit_length() - 1
    if n_seg != 2 or n_dp != 1 << bits or bits < 2 or rows % 64:
        return None
    rows, dims = rows // 4, []
    for _ in range(bits):
        if cols % 256 == 0:
            cols, dims = cols // 2, dims + [1]
        elif rows % 32 == 0:
            rows, dims = rows // 2, dims + [0]
        else:
            return None
    order = list(range(bits))
    return [list(zip(order, dims)), list(zip([1, 0] + order[2:], dims))]


def region(ref, at, shape):
    return ref.at[
        pl.ds(pl.multiple_of(at[0], 16), shape[0]), pl.ds(pl.multiple_of(at[1], 128), shape[1])
    ]


def stage_shapes(shape, plan):
    shapes = []
    for _, dim in plan:
        shape = (shape[0] // 2, shape[1]) if dim == 0 else (shape[0], shape[1] // 2)
        shapes.append(shape)
    return shapes


def by_rows(rows, body):
    block = next(size for size in (80, 64, 48, 32, 16) if rows % size == 0)

    @pl.loop(0, rows // block)
    def _(i):
        body(pl.multiple_of(i * block, BLOCK), block)


def sum_kernel(plans, attn_ref, grad_ref, out_ref, acc, core_out, core_in, gath, square_out, square_in, *rest):
    n_bits = len(plans[0])
    parts = len(plans)
    sends = [rest[p * n_bits : (p + 1) * n_bits] for p in range(parts)]
    recvs = [rest[(parts + p) * n_bits : (parts + p + 1) * n_bits] for p in range(parts)]
    send_sem, recv_sem = rest[2 * parts * n_bits :]
    seg, dp = lax.axis_index("seg"), lax.axis_index("dp")
    half, cols = acc.shape
    bit = [dp // (1 << b) % 2 for b in range(n_bits)]
    partner = [(seg, dp + (1 << b) * (1 - 2 * bit[b])) for b in range(n_bits)]
    other = (1 - seg, dp)
    count = [0]

    def send(source, target, device):
        at = count[0]
        count[0] += 1
        copy = pltpu.make_async_remote_copy(
            src_ref=source,
            dst_ref=target,
            send_sem=send_sem.at[at],
            recv_sem=recv_sem.at[at],
            device_id=device,
            device_id_type=pl.DeviceIdType.MESH,
        )
        copy.start()
        return copy

    barrier = pltpu.get_barrier_semaphore()
    for device in [other] + partner:
        pl.semaphore_signal(barrier, inc=1, device_id=device, device_id_type=pl.DeviceIdType.MESH)
    pl.semaphore_wait(barrier, 1 + n_bits)

    pieces = 4
    piece = half // pieces
    core = []
    for i in range(pieces):
        rows = pl.ds(pl.multiple_of((1 - seg) * half + i * piece, BLOCK), piece)
        core_out[i] = dot(attn_ref[rows, :], grad_ref[...], ((1,), (0,))).astype(jnp.bfloat16)
        core.append(send(core_out.at[i], core_in.at[i], other))
    for i in range(pieces):
        rows = pl.ds(pl.multiple_of(seg * half + i * piece, BLOCK), piece)
        acc[i * piece : (i + 1) * piece, :] = dot(attn_ref[rows, :], grad_ref[...], ((1,), (0,)))
    for i in range(pieces):
        core[i].wait()

        def add(row, block):
            acc[pl.ds(i * piece + row, block), :] += core_in[i, pl.ds(row, block), :].astype(
                jnp.float32
            )

        by_rows(piece, add)

    places = [(p * (half // parts), 0) for p in range(parts)]
    history = [[] for _ in range(parts)]
    for stage in range(n_bits):
        copies = []
        for p in range(parts):
            b, dim = plans[p][stage]
            shape = sends[p][stage].shape
            at = places[p]
            step = shape[dim]
            keep, give = [
                tuple(at[d] + (which * step if d == dim else 0) for d in range(2))
                for which in (bit[b], 1 - bit[b])
            ]
            lanes = pl.ds(pl.multiple_of(give[1], 128), shape[1])

            def cast(row, block):
                rows = pl.ds(pl.multiple_of(give[0] + row, BLOCK), block)
                sends[p][stage][pl.ds(row, block), :] = acc[rows, lanes].astype(jnp.bfloat16)

            by_rows(shape[0], cast)
            copies.append(send(sends[p][stage], recvs[p][stage], partner[b]))
            history[p].append((b, keep, shape))
            places[p] = keep
        for p in range(parts):
            copies[p].wait()
            _, keep, shape = history[p][stage]
            lanes = pl.ds(pl.multiple_of(keep[1], 128), shape[1])

            def add(row, block):
                rows = pl.ds(pl.multiple_of(keep[0] + row, BLOCK), block)
                acc[rows, lanes] += recvs[p][stage][pl.ds(row, block), :].astype(jnp.float32)

            by_rows(shape[0], add)

    squares = jnp.zeros((1, 1), jnp.float32)
    for p in range(parts):
        _, keep, shape = history[p][-1]
        own = region(acc, keep, shape)[...]
        squares = squares + jnp.sum(own * own, keepdims=True)
        region(gath, (seg * half + keep[0], keep[1]), shape)[...] = own.astype(jnp.bfloat16)
    square_out[0] = jnp.broadcast_to(squares, square_out.shape[1:])

    for stage in reversed(range(n_bits)):
        step = n_bits - 1 - stage
        copies = [send(square_out.at[step], square_in.at[step], partner[plans[0][stage][0]])]
        for p in range(parts):
            b, keep, shape = history[p][stage]
            mine = region(gath, (seg * half + keep[0], keep[1]), shape)
            copies.append(send(mine, mine, partner[b]))
        for copy in copies:
            copy.wait()
        square_out[step + 1] = square_out[step] + square_in[step]
    step = n_bits
    copies = [send(square_out.at[step], square_in.at[step], other)]
    mine = gath.at[pl.ds(pl.multiple_of(seg * half, BLOCK), half), :]
    copies.append(send(mine, mine, other))
    for copy in copies:
        copy.wait()
    total = square_out[step] + square_in[step]
    rms = jnp.sqrt(total[:1, :1] / (2 * half * cols) + 1e-06)
    factor = jnp.minimum(1.0, 1.0 / rms)

    def finish(row, block):
        rows = pl.ds(row, block)
        out_ref[rows, :] = (gath[rows, :].astype(jnp.float32) * factor).astype(jnp.bfloat16)

    by_rows(2 * half, finish)


def sum_weight(n_seg, n_dp, plans, attn_t, out_grad):
    width, cols = attn_t.shape[0], out_grad.shape[1]
    half, bits = width // 2, len(plans[0])
    low = functools.partial(pltpu.VMEM, dtype=jnp.bfloat16)
    shapes = [stage_shapes((half // len(plans), cols), plan) for plan in plans]
    buffers = [low(shape) for part in shapes for shape in part]
    copies = 4 + len(plans) * bits + (len(plans) + 1) * bits + 2
    vmem = pl.BlockSpec(memory_space=pltpu.VMEM)
    return pl.pallas_call(
        functools.partial(sum_kernel, plans),
        in_specs=[vmem] * 2,
        out_specs=vmem,
        out_shape=jax.ShapeDtypeStruct((width, cols), jnp.bfloat16),
        scratch_shapes=[
            pltpu.VMEM((half, cols), jnp.float32),
            low((4, half // 4, cols)),
            low((4, half // 4, cols)),
            low((width, cols)),
            pltpu.VMEM((bits + 1, 8, 128), jnp.float32),
            pltpu.VMEM((bits + 1, 8, 128), jnp.float32),
            *buffers,
            *buffers,
            pltpu.SemaphoreType.DMA((copies,)),
            pltpu.SemaphoreType.DMA((copies,)),
        ],
        compiler_params=pltpu.CompilerParams(
            collective_id=0, has_side_effects=True, vmem_limit_bytes=56 * 1024 * 1024
        ),
        cost_estimate=pl.CostEstimate(
            flops=2 * width * cols * attn_t.shape[1],
            bytes_accessed=4 * width * cols,
            transcendentals=0,
        ),
    )(attn_t, out_grad)


def solution(mesh):
    row = P("dp", "seg", None)
    return jax.shard_map(
        functools.partial(shards, mesh.shape["seg"], mesh.shape["dp"]),
        mesh=mesh,
        in_specs=(row,) * 6 + (P(),),
        out_specs=(row,) * 5 + (P(),),
        check_vma=False,
    )
```

```python
import functools

import jax
import jax.numpy as jnp
from jax import lax
from jax.experimental import pallas as pl
from jax.experimental.pallas import tpu as pltpu
from jax.sharding import PartitionSpec as P

HEADS = 16
GROUP = 8
BLOCK = 16
LOG2E = 1.4426950408889634


def dot(a, b, contract):
    return lax.dot_general(a, b, (contract, ((), ())), preferred_element_type=jnp.float32)


def hidden(pad, prefix_visible, keys, first_query, queries):
    rows = lax.broadcasted_iota(jnp.int32, (keys, queries), 0)
    cols = lax.broadcasted_iota(jnp.int32, (keys, queries), 1) + first_query
    return jnp.where(rows < pad, rows + 1 - prefix_visible, rows - pad - cols) > 0


def spans(tokens):
    size = tokens // 2 if tokens % 256 == 0 else tokens
    return [(start, size) for start in range(0, tokens, size)]


def fwd_kernel(sums, head_size, q_ref, k_ref, v_ref, pk_ref, pv_ref, attn_ref, max_ref, inv_ref):
    tokens, pad = q_ref.shape[0], pk_ref.shape[0]
    visible = lax.axis_index("seg") * sums
    scale = head_size**-0.5 * LOG2E
    for start, size in spans(tokens):
        own = start + size
        mask = hidden(pad, visible, pad + own, start, size)
        for head in range(q_ref.shape[1] // head_size):
            lanes = slice(head * head_size, (head + 1) * head_size)
            keys = jnp.concatenate([pk_ref[:, lanes], k_ref[:own, lanes]], 0)
            values = jnp.concatenate([pv_ref[:, lanes], v_ref[:own, lanes]], 0)
            scores = dot(keys, q_ref[start:own, lanes], ((1,), (1,)))
            scores = jnp.where(mask, jnp.float32(-1e30), scores)
            top = jnp.max(scores, 0, keepdims=True)
            weights = jnp.exp2((scores - top) * scale)
            inverse = 1.0 / jnp.sum(weights, 0, keepdims=True)
            probs_low = (weights * inverse).astype(jnp.bfloat16)
            attn = dot(values, probs_low, ((0,), (0,)))
            attn_ref[lanes, start:own] = attn.astype(jnp.bfloat16)
            max_ref[head : head + 1, start:own] = top
            inv_ref[head : head + 1, start:own] = inverse


def bwd_kernel(
    sums,
    head_size,
    q_ref,
    k_ref,
    v_ref,
    pk_ref,
    pv_ref,
    g_ref,
    max_ref,
    inv_ref,
    dq_ref,
    dk_ref,
    dv_ref,
    dpk_ref,
    dpv_ref,
    dq_t,
):
    tokens, pad = q_ref.shape[0], pk_ref.shape[0]
    visible = lax.axis_index("seg") * sums
    scaling = head_size**-0.5
    parts = spans(tokens)
    masks = [hidden(pad, visible, pad + start + size, start, size) for start, size in parts]
    for head in range(q_ref.shape[1] // head_size):
        lanes = slice(head * head_size, (head + 1) * head_size)
        key_sum, value_sum = [], []
        for (start, size), mask in zip(parts, masks):
            own = start + size
            keys = jnp.concatenate([pk_ref[:, lanes], k_ref[:own, lanes]], 0)
            values = jnp.concatenate([pv_ref[:, lanes], v_ref[:own, lanes]], 0)
            query, grad = q_ref[start:own, lanes], g_ref[start:own, lanes]
            scores = dot(keys, query, ((1,), (1,)))
            scores = jnp.where(mask, jnp.float32(-1e30), scores)
            top = max_ref[head : head + 1, start:own]
            inverse = inv_ref[head : head + 1, start:own]
            probs = jnp.exp2((scores - top) * (scaling * LOG2E)) * inverse
            prob_grad = dot(values, grad, ((1,), (1,)))
            weighted = probs * prob_grad
            row_delta = jnp.sum(weighted, 0, keepdims=True)
            score_grad = (scaling * (weighted - probs * row_delta)).astype(jnp.bfloat16)
            probs_low = probs.astype(jnp.bfloat16)
            dq_t[lanes, start:own] = dot(keys, score_grad, ((0,), (0,)))
            key_sum.append(dot(score_grad, query, ((1,), (0,))))
            value_sum.append(dot(probs_low, grad, ((1,), (0,))))
        for sum_list, own_ref, prompt_ref in (
            (key_sum, dk_ref, dpk_ref),
            (value_sum, dv_ref, dpv_ref),
        ):
            total = sum_list[-1]
            for part in sum_list[:-1]:
                count = part.shape[0]
                total = jnp.concatenate([total[:count] + part, total[count:]], 0)
            prompt_ref[:, lanes] = total[:pad].astype(jnp.bfloat16)
            own_ref[:, lanes] = total[pad:].astype(jnp.bfloat16)
    dq_ref[...] = dq_t[...].T.astype(jnp.bfloat16)


def lanes_block(rows, width):
    return pl.BlockSpec((rows, width), lambda g: (0, g))


def rows_block(rows, width):
    return pl.BlockSpec((rows, width), lambda g: (g, 0))


def shards(n_seg, n_dp, query, key, value, prompt_keys, prompt_values, out_grad, w_out):
    query, key, value, out_grad = query[0], key[0], value[0], out_grad[0]
    tokens, width = query.shape
    sums = prompt_keys.shape[1]
    head_size = width // HEADS
    group = GROUP * head_size
    read = (n_seg - 1) * sums
    pad = -(-read // 64) * 64
    prompts = jnp.stack([prompt_keys[0], prompt_values[0]])
    prompts = lax.all_gather(prompts, "seg", axis=1, tiled=True)[:, :read]
    prompts = jnp.pad(prompts, ((0, 0), (0, pad - read), (0, 0)))
    prompt_k, prompt_v = prompts[0], prompts[1]
    params = pltpu.CompilerParams(vmem_limit_bytes=48 * 1024 * 1024)
    own_spec, prompt_spec = lanes_block(tokens, group), lanes_block(pad, group)
    stat_spec = rows_block(GROUP, tokens)
    stat = jax.ShapeDtypeStruct((HEADS, tokens), jnp.float32)
    low = functools.partial(jax.ShapeDtypeStruct, dtype=jnp.bfloat16)
    flops = 2 * HEADS * tokens * tokens * head_size

    attn_t, top, inverse = pl.pallas_call(
        functools.partial(fwd_kernel, sums, head_size),
        grid=(HEADS // GROUP,),
        in_specs=[own_spec] * 3 + [prompt_spec] * 2,
        out_specs=[rows_block(group, tokens), stat_spec, stat_spec],
        out_shape=[low((width, tokens)), stat, stat],
        compiler_params=params,
        cost_estimate=pl.CostEstimate(
            flops=10 * flops, bytes_accessed=8 * tokens * width, transcendentals=0
        ),
    )(query, key, value, prompt_k, prompt_v)

    plan = split_plan(n_seg, n_dp, width, out_grad.shape[1])
    if plan is None:
        weight_grad = plain_weight(attn_t, out_grad)
    else:
        weight_grad = sum_weight(n_seg, n_dp, plan, attn_t, out_grad)

    head_low = jnp.einsum("td,hd->th", out_grad, w_out, preferred_element_type=jnp.float32)
    query_grad, key_grad, value_grad, pk_part, pv_part = pl.pallas_call(
        functools.partial(bwd_kernel, sums, head_size),
        grid=(HEADS // GROUP,),
        in_specs=[own_spec] * 3 + [prompt_spec] * 2 + [own_spec, stat_spec, stat_spec],
        out_specs=[own_spec] * 3 + [prompt_spec] * 2,
        out_shape=[low((tokens, width))] * 3 + [low((pad, width))] * 2,
        scratch_shapes=[pltpu.VMEM((group, tokens), jnp.float32)],
        compiler_params=params,
        cost_estimate=pl.CostEstimate(
            flops=25 * flops, bytes_accessed=16 * tokens * width, transcendentals=0
        ),
    )(query, key, value, prompt_k, prompt_v, head_low.astype(jnp.bfloat16), top, inverse)

    parts = jnp.stack([pk_part, pv_part])
    segment = lax.axis_index("seg")
    later = jnp.zeros((2, sums, width), jnp.float32)
    for step in range(1, n_seg):
        start = jnp.maximum(segment - step, 0) * sums
        block = lax.dynamic_slice_in_dim(parts, start, sums, 1)
        pairs = [(at, at - step) for at in range(step, n_seg)]
        later = later + lax.ppermute(block, "seg", pairs).astype(jnp.float32)
    later = later.astype(jnp.bfloat16)

    return (
        query_grad[None],
        key_grad[None],
        value_grad[None],
        later[0][None],
        later[1][None],
        weight_grad,
    )


def plain_weight(attn_t, out_grad):
    part = jnp.dot(attn_t, out_grad, preferred_element_type=jnp.float32)
    total = lax.psum(part, ("seg", "dp"))
    rms = jnp.sqrt(jnp.mean(total * total) + 1e-06)
    return (total * jnp.minimum(1.0, 1.0 / rms)).astype(jnp.bfloat16)


def split_plan(n_seg, n_dp, rows, cols):
    bits = n_dp.bit_length() - 1
    if n_seg != 2 or n_dp != 1 << bits or bits < 3:
        return None
    order = list(range(bits))
    orders = [order, [1, 0] + order[2:], [2, 0, 1] + order[3:]]
    for parts in (5, 4, 3, 2, 1):
        size, width, dims = rows // (2 * parts), cols, []
        if rows % (2 * parts * BLOCK):
            continue
        for _ in range(bits):
            if width % 256 == 0:
                width, dims = width // 2, dims + [1]
            elif size % (2 * BLOCK) == 0:
                size, dims = size // 2, dims + [0]
        if len(dims) == bits:
            return [list(zip(orders[part % 3], dims)) for part in range(parts)]
    return None


def region(ref, at, shape):
    return ref.at[
        pl.ds(pl.multiple_of(at[0], 16), shape[0]), pl.ds(pl.multiple_of(at[1], 128), shape[1])
    ]


def stage_shapes(shape, plan):
    shapes = []
    for _, dim in plan:
        shape = (shape[0] // 2, shape[1]) if dim == 0 else (shape[0], shape[1] // 2)
        shapes.append(shape)
    return shapes


def by_rows(rows, body):
    block = next(size for size in (64, 48, 32, 16) if rows % size == 0)

    @pl.loop(0, rows // block)
    def _(i):
        body(pl.multiple_of(i * block, BLOCK), block)


def sum_kernel(plans, attn_ref, grad_ref, out_ref, square_ref, acc, core_out, core_in, gath, square_out, square_in, *rest):
    n_bits = len(plans[0])
    parts = len(plans)
    sends = [rest[p * n_bits : (p + 1) * n_bits] for p in range(parts)]
    recvs = [rest[(parts + p) * n_bits : (parts + p + 1) * n_bits] for p in range(parts)]
    send_sem, recv_sem, local_sem = rest[2 * parts * n_bits :]
    seg, dp = lax.axis_index("seg"), lax.axis_index("dp")
    half = acc.shape[0]
    size = half // parts
    bit = [dp // (1 << b) % 2 for b in range(n_bits)]
    partner = [(seg, dp + (1 << b) * (1 - 2 * bit[b])) for b in range(n_bits)]
    other = (1 - seg, dp)
    count = [0, 0]

    def send(source, target, device):
        at = count[0]
        count[0] += 1
        copy = pltpu.make_async_remote_copy(
            src_ref=source,
            dst_ref=target,
            send_sem=send_sem.at[at],
            recv_sem=recv_sem.at[at],
            device_id=device,
            device_id_type=pl.DeviceIdType.MESH,
        )
        copy.start()
        return copy

    def part_rows(side, p):
        return pl.ds(pl.multiple_of(side * half + p * size, BLOCK), size)

    def store(side, p):
        at = count[1]
        count[1] += 1
        rows = part_rows(side, p)
        copy = pltpu.make_async_copy(gath.at[rows, :], out_ref.at[rows, :], local_sem.at[at])
        copy.start()
        return copy

    barrier = pltpu.get_barrier_semaphore()
    for device in [other] + partner:
        pl.semaphore_signal(barrier, inc=1, device_id=device, device_id_type=pl.DeviceIdType.MESH)
    pl.semaphore_wait(barrier, 1 + n_bits)

    core = []
    for p in range(parts):
        product = dot(attn_ref[part_rows(1 - seg, p), :], grad_ref[...], ((1,), (0,)))
        core_out[p] = product.astype(jnp.bfloat16)
        core.append(send(core_out.at[p], core_in.at[p], other))
    places = [(p * size, 0) for p in range(parts)]
    history = [[] for _ in range(parts)]
    flying = [None] * parts
    for stage in range(n_bits):
        for p in range(parts):
            if stage == 0:
                acc[p * size : (p + 1) * size, :] = dot(
                    attn_ref[part_rows(seg, p), :], grad_ref[...], ((1,), (0,))
                )
                core[p].wait()
                arrived, at, shape = core_in.at[p], places[p], (size, acc.shape[1])
            else:
                flying[p].wait()
                arrived, (_, at, shape) = recvs[p][stage - 1], history[p][-1]
            add_arrived(acc, arrived, at, shape)
            b, dim = plans[p][stage]
            shape = sends[p][stage].shape
            keep, give = [
                tuple(at[d] + (which * shape[d] if d == dim else 0) for d in range(2))
                for which in (bit[b], 1 - bit[b])
            ]
            cast_given(acc, sends[p][stage], give, shape)
            flying[p] = send(sends[p][stage], recvs[p][stage], partner[b])
            history[p].append((b, keep, shape))

    def gather(p, stage):
        b, keep, shape = history[p][stage]
        mine = region(gath, (seg * half + keep[0], keep[1]), shape)
        return send(mine, mine, partner[b])

    squares = jnp.zeros((1, 1), jnp.float32)
    for p in range(parts):
        flying[p].wait()
        _, keep, shape = history[p][-1]
        own = region(acc, keep, shape)[...] + recvs[p][-1][...].astype(jnp.float32)
        squares = squares + jnp.sum(own * own, keepdims=True)
        region(gath, (seg * half + keep[0], keep[1]), shape)[...] = own.astype(jnp.bfloat16)
        flying[p] = gather(p, n_bits - 1)
    square_out[0] = jnp.broadcast_to(squares, square_out.shape[1:])
    square_copy = send(square_out.at[0], square_in.at[0], partner[0])

    stores = []
    for stage in reversed(range(n_bits)):
        for p in range(parts):
            flying[p].wait()
            if stage > 0:
                flying[p] = gather(p, stage - 1)
            else:
                mine = gath.at[part_rows(seg, p), :]
                flying[p] = send(mine, mine, other)
                stores.append(store(seg, p))
        step = n_bits - 1 - stage
        square_copy.wait()
        square_out[step + 1] = square_out[step] + square_in[step]
        device = partner[step + 1] if step + 1 < n_bits else other
        square_copy = send(square_out.at[step + 1], square_in.at[step + 1], device)
    square_copy.wait()
    square_ref[...] = square_out[n_bits] + square_in[n_bits]
    for p in range(parts):
        flying[p].wait()
        stores.append(store(1 - seg, p))
    for copy in stores:
        copy.wait()


def add_arrived(acc, arrived, at, shape):
    lanes = pl.ds(pl.multiple_of(at[1], 128), shape[1])

    def add(row, block):
        rows = pl.ds(pl.multiple_of(at[0] + row, BLOCK), block)
        acc[rows, lanes] += arrived[pl.ds(row, block), :].astype(jnp.float32)

    by_rows(shape[0], add)


def cast_given(acc, target, at, shape):
    lanes = pl.ds(pl.multiple_of(at[1], 128), shape[1])

    def cast(row, block):
        rows = pl.ds(pl.multiple_of(at[0] + row, BLOCK), block)
        target[pl.ds(row, block), :] = acc[rows, lanes].astype(jnp.bfloat16)

    by_rows(shape[0], cast)


def sum_weight(n_seg, n_dp, plans, attn_t, out_grad):
    width, cols = attn_t.shape[0], out_grad.shape[1]
    half, bits, parts = width // 2, len(plans[0]), len(plans)
    low = functools.partial(pltpu.VMEM, dtype=jnp.bfloat16)
    shapes = [stage_shapes((half // parts, cols), plan) for plan in plans]
    buffers = [low(shape) for part in shapes for shape in part]
    copies = 2 * parts + 2 * parts * bits + bits + 1
    vmem = pl.BlockSpec(memory_space=pltpu.VMEM)
    total, squares = pl.pallas_call(
        functools.partial(sum_kernel, plans),
        in_specs=[vmem] * 2,
        out_specs=[pl.BlockSpec(memory_space=pl.ANY), vmem],
        out_shape=[
            jax.ShapeDtypeStruct((width, cols), jnp.bfloat16),
            jax.ShapeDtypeStruct((8, 128), jnp.float32),
        ],
        scratch_shapes=[
            pltpu.VMEM((half, cols), jnp.float32),
            low((parts, half // parts, cols)),
            low((parts, half // parts, cols)),
            low((width, cols)),
            pltpu.VMEM((bits + 1, 8, 128), jnp.float32),
            pltpu.VMEM((bits + 1, 8, 128), jnp.float32),
            *buffers,
            *buffers,
            pltpu.SemaphoreType.DMA((copies,)),
            pltpu.SemaphoreType.DMA((copies,)),
            pltpu.SemaphoreType.DMA((2 * parts,)),
        ],
        compiler_params=pltpu.CompilerParams(
            collective_id=0, has_side_effects=True, vmem_limit_bytes=56 * 1024 * 1024
        ),
        cost_estimate=pl.CostEstimate(
            flops=2 * width * cols * attn_t.shape[1],
            bytes_accessed=4 * width * cols,
            transcendentals=0,
        ),
    )(attn_t, out_grad)
    rms = jnp.sqrt(squares[0, 0] / (width * cols) + 1e-06)
    return (total.astype(jnp.float32) * jnp.minimum(1.0, 1.0 / rms)).astype(jnp.bfloat16)


def solution(mesh):
    row = P("dp", "seg", None)
    return jax.shard_map(
        functools.partial(shards, mesh.shape["seg"], mesh.shape["dp"]),
        mesh=mesh,
        in_specs=(row,) * 6 + (P(),),
        out_specs=(row,) * 5 + (P(),),
        check_vma=False,
    )
```

```python
import functools

import jax
import jax.numpy as jnp
from jax import lax
from jax.experimental import pallas as pl
from jax.experimental.pallas import tpu as pltpu
from jax.sharding import PartitionSpec as P

HEADS = 16
GROUP = 8
BLOCK = 16
LOG2E = 1.4426950408889634


def dot(a, b, contract):
    return lax.dot_general(a, b, (contract, ((), ())), preferred_element_type=jnp.float32)


def hidden(pad, prefix_visible, keys, first_query, queries):
    rows = lax.broadcasted_iota(jnp.int32, (keys, queries), 0)
    cols = lax.broadcasted_iota(jnp.int32, (keys, queries), 1) + first_query
    return jnp.where(rows < pad, rows + 1 - prefix_visible, rows - pad - cols) > 0


def spans(tokens):
    size = tokens // 2 if tokens % 256 == 0 else tokens
    return [(start, size) for start in range(0, tokens, size)]


def fwd_kernel(sums, head_size, q_ref, k_ref, v_ref, pk_ref, pv_ref, attn_ref, max_ref, inv_ref):
    tokens, pad = q_ref.shape[0], pk_ref.shape[0]
    visible = lax.axis_index("seg") * sums
    scale = head_size**-0.5 * LOG2E
    for start, size in spans(tokens):
        own = start + size
        mask = hidden(pad, visible, pad + own, start, size)
        for head in range(q_ref.shape[1] // head_size):
            lanes = slice(head * head_size, (head + 1) * head_size)
            keys = jnp.concatenate([pk_ref[:, lanes], k_ref[:own, lanes]], 0)
            values = jnp.concatenate([pv_ref[:, lanes], v_ref[:own, lanes]], 0)
            scores = dot(keys, q_ref[start:own, lanes], ((1,), (1,)))
            scores = jnp.where(mask, jnp.float32(-1e30), scores)
            top = jnp.max(scores, 0, keepdims=True)
            weights = jnp.exp2((scores - top) * scale)
            inverse = 1.0 / jnp.sum(weights, 0, keepdims=True)
            probs_low = (weights * inverse).astype(jnp.bfloat16)
            attn = dot(values, probs_low, ((0,), (0,)))
            attn_ref[lanes, start:own] = attn.astype(jnp.bfloat16)
            max_ref[head : head + 1, start:own] = top
            inv_ref[head : head + 1, start:own] = inverse


def bwd_head(sums, head_size, head, refs):
    q_ref, k_ref, v_ref, pk_ref, pv_ref, g_ref, max_ref, inv_ref = refs[:8]
    dk_ref, dv_ref, dpk_ref, dpv_ref, dq_t = refs[8:]
    tokens, pad = q_ref.shape[0], pk_ref.shape[0]
    visible = lax.axis_index("seg") * sums
    scaling = head_size**-0.5
    parts = spans(tokens)
    masks = [hidden(pad, visible, pad + start + size, start, size) for start, size in parts]
    lanes = slice(head * head_size, (head + 1) * head_size)
    key_sum, value_sum = [], []
    for (start, size), mask in zip(parts, masks):
        own = start + size
        keys = jnp.concatenate([pk_ref[:, lanes], k_ref[:own, lanes]], 0)
        values = jnp.concatenate([pv_ref[:, lanes], v_ref[:own, lanes]], 0)
        query, grad = q_ref[start:own, lanes], g_ref[start:own, lanes]
        scores = dot(keys, query, ((1,), (1,)))
        scores = jnp.where(mask, jnp.float32(-1e30), scores)
        top = max_ref[head : head + 1, start:own]
        inverse = inv_ref[head : head + 1, start:own]
        probs = jnp.exp2((scores - top) * (scaling * LOG2E)) * inverse
        prob_grad = dot(values, grad, ((1,), (1,)))
        weighted = probs * prob_grad
        row_delta = jnp.sum(weighted, 0, keepdims=True)
        score_grad = (scaling * (weighted - probs * row_delta)).astype(jnp.bfloat16)
        probs_low = probs.astype(jnp.bfloat16)
        dq_t[lanes, start:own] = dot(keys, score_grad, ((0,), (0,)))
        key_sum.append(dot(score_grad, query, ((1,), (0,))))
        value_sum.append(dot(probs_low, grad, ((1,), (0,))))
    for sum_list, own_ref, prompt_ref in (
        (key_sum, dk_ref, dpk_ref),
        (value_sum, dv_ref, dpv_ref),
    ):
        total = sum_list[-1]
        for part in sum_list[:-1]:
            count = part.shape[0]
            total = jnp.concatenate([total[:count] + part, total[count:]], 0)
        prompt_ref[:, lanes] = total[:pad].astype(jnp.bfloat16)
        own_ref[:, lanes] = total[pad:].astype(jnp.bfloat16)


def bwd_kernel(sums, head_size, *refs):
    dq_ref, dq_t = refs[8], refs[13]
    for head in range(refs[0].shape[1] // head_size):
        bwd_head(sums, head_size, head, refs[:8] + refs[9:])
    dq_ref[...] = dq_t[...].T.astype(jnp.bfloat16)


def lanes_block(rows, width):
    return pl.BlockSpec((rows, width), lambda g: (0, g))


def rows_block(rows, width):
    return pl.BlockSpec((rows, width), lambda g: (g, 0))


def shards(n_seg, n_dp, query, key, value, prompt_keys, prompt_values, out_grad, w_out):
    query, key, value, out_grad = query[0], key[0], value[0], out_grad[0]
    tokens, width = query.shape
    sums = prompt_keys.shape[1]
    head_size = width // HEADS
    group = GROUP * head_size
    read = (n_seg - 1) * sums
    pad = -(-read // 64) * 64
    prompts = jnp.stack([prompt_keys[0], prompt_values[0]])
    prompts = lax.all_gather(prompts, "seg", axis=1, tiled=True)[:, :read]
    prompts = jnp.pad(prompts, ((0, 0), (0, pad - read), (0, 0)))
    prompt_k, prompt_v = prompts[0], prompts[1]
    params = pltpu.CompilerParams(vmem_limit_bytes=48 * 1024 * 1024)
    own_spec, prompt_spec = lanes_block(tokens, group), lanes_block(pad, group)
    stat_spec = rows_block(GROUP, tokens)
    stat = jax.ShapeDtypeStruct((HEADS, tokens), jnp.float32)
    low = functools.partial(jax.ShapeDtypeStruct, dtype=jnp.bfloat16)
    flops = 2 * HEADS * tokens * tokens * head_size

    attn_t, top, inverse = pl.pallas_call(
        functools.partial(fwd_kernel, sums, head_size),
        grid=(HEADS // GROUP,),
        in_specs=[own_spec] * 3 + [prompt_spec] * 2,
        out_specs=[rows_block(group, tokens), stat_spec, stat_spec],
        out_shape=[low((width, tokens)), stat, stat],
        compiler_params=params,
        cost_estimate=pl.CostEstimate(
            flops=10 * flops, bytes_accessed=8 * tokens * width, transcendentals=0
        ),
    )(query, key, value, prompt_k, prompt_v)

    plan = split_plan(n_seg, n_dp, width, out_grad.shape[1])
    shapes = [low((tokens, width))] * 3 + [low((pad, width))] * 2
    if plan is None:
        weight_grad = plain_weight(attn_t, out_grad)
        head_low = jnp.einsum("td,hd->th", out_grad, w_out, preferred_element_type=jnp.float32)
        query_grad, key_grad, value_grad, pk_part, pv_part = pl.pallas_call(
            functools.partial(bwd_kernel, sums, head_size),
            grid=(HEADS // GROUP,),
            in_specs=[own_spec] * 3 + [prompt_spec] * 2 + [own_spec, stat_spec, stat_spec],
            out_specs=[own_spec] * 3 + [prompt_spec] * 2,
            out_shape=shapes,
            scratch_shapes=[pltpu.VMEM((group, tokens), jnp.float32)],
            compiler_params=params,
            cost_estimate=pl.CostEstimate(
                flops=25 * flops, bytes_accessed=16 * tokens * width, transcendentals=0
            ),
        )(query, key, value, prompt_k, prompt_v, head_low.astype(jnp.bfloat16), top, inverse)
    else:
        operands = (query, key, value, prompt_k, prompt_v, top, inverse)
        outs = sum_weight(sums, head_size, plan, attn_t, out_grad, w_out, operands, shapes)
        query_grad, key_grad, value_grad, pk_part, pv_part, weight_grad = outs

    parts = jnp.stack([pk_part, pv_part])
    segment = lax.axis_index("seg")
    later = jnp.zeros((2, sums, width), jnp.float32)
    for step in range(1, n_seg):
        start = jnp.maximum(segment - step, 0) * sums
        block = lax.dynamic_slice_in_dim(parts, start, sums, 1)
        pairs = [(at, at - step) for at in range(step, n_seg)]
        later = later + lax.ppermute(block, "seg", pairs).astype(jnp.float32)
    later = later.astype(jnp.bfloat16)

    return (
        query_grad[None],
        key_grad[None],
        value_grad[None],
        later[0][None],
        later[1][None],
        weight_grad,
    )


def plain_weight(attn_t, out_grad):
    part = jnp.dot(attn_t, out_grad, preferred_element_type=jnp.float32)
    total = lax.psum(part, ("seg", "dp"))
    rms = jnp.sqrt(jnp.mean(total * total) + 1e-06)
    return (total * jnp.minimum(1.0, 1.0 / rms)).astype(jnp.bfloat16)


def split_plan(n_seg, n_dp, rows, cols):
    bits = n_dp.bit_length() - 1
    if n_seg != 2 or n_dp != 1 << bits or bits < 3:
        return None
    order = list(range(bits))
    orders = [order, [1, 0] + order[2:], [2, 0, 1] + order[3:]]
    for parts in (5, 4, 3, 2, 1):
        size, width, dims = rows // (2 * parts), cols, []
        if rows % (2 * parts * BLOCK):
            continue
        for _ in range(bits):
            if width % 256 == 0:
                width, dims = width // 2, dims + [1]
            elif size % (2 * BLOCK) == 0:
                size, dims = size // 2, dims + [0]
        if len(dims) == bits:
            return [list(zip(orders[part % 3], dims)) for part in range(parts)]
    return None


def region(ref, at, shape):
    return ref.at[
        pl.ds(pl.multiple_of(at[0], 16), shape[0]), pl.ds(pl.multiple_of(at[1], 128), shape[1])
    ]


def stage_shapes(shape, plan):
    shapes = []
    for _, dim in plan:
        shape = (shape[0] // 2, shape[1]) if dim == 0 else (shape[0], shape[1] // 2)
        shapes.append(shape)
    return shapes


def by_rows(rows, body):
    block = next(size for size in (64, 48, 32, 16) if rows % size == 0)

    @pl.loop(0, rows // block)
    def _(i):
        body(pl.multiple_of(i * block, BLOCK), block)


def sum_kernel(plans, sums, head_size, *refs):
    attn_ref, grad_ref, w_hbm = refs[:3]
    own_refs, (max_ref, inv_ref) = refs[3:8], refs[8:10]
    out_ref, square_ref, dq_ref, dk_ref, dv_ref, dpk_ref, dpv_ref = refs[10:17]
    acc, core_out, core_in, gath, square_out, square_in, w_ref, g_ref, dq_t = refs[17:26]
    rest = refs[26:]
    n_bits = len(plans[0])
    parts = len(plans)
    sends = [rest[p * n_bits : (p + 1) * n_bits] for p in range(parts)]
    recvs = [rest[(parts + p) * n_bits : (parts + p + 1) * n_bits] for p in range(parts)]
    send_sem, recv_sem, local_sem = rest[2 * parts * n_bits :]
    seg, dp = lax.axis_index("seg"), lax.axis_index("dp")
    half = acc.shape[0]
    size = half // parts
    bit = [dp // (1 << b) % 2 for b in range(n_bits)]
    partner = [(seg, dp + (1 << b) * (1 - 2 * bit[b])) for b in range(n_bits)]
    other = (1 - seg, dp)
    count = [0, 0]

    def send(source, target, device):
        at = count[0]
        count[0] += 1
        copy = pltpu.make_async_remote_copy(
            src_ref=source,
            dst_ref=target,
            send_sem=send_sem.at[at],
            recv_sem=recv_sem.at[at],
            device_id=device,
            device_id_type=pl.DeviceIdType.MESH,
        )
        copy.start()
        return copy

    def head_grad(start, stop):
        g_ref[:, start:stop] = dot(grad_ref[...], w_ref[start:stop, :], ((1,), (1,))).astype(
            jnp.bfloat16
        )

    width = w_ref.shape[0]
    chunk = 256 if width % 256 == 0 else width
    chunks = [functools.partial(head_grad, at, at + chunk) for at in range(0, width, chunk)]
    head_refs = own_refs + (g_ref, max_ref, inv_ref, dk_ref, dv_ref, dpk_ref, dpv_ref, dq_t)
    heads = [
        functools.partial(bwd_head, sums, head_size, head, head_refs) for head in range(HEADS)
    ]
    turns = [0]

    def work():
        turns[0] += 1
        if turns[0] % 2 and heads:
            heads.pop(0)()

    def part_rows(side, p):
        return pl.ds(pl.multiple_of(side * half + p * size, BLOCK), size)

    def store(side, p):
        at = count[1]
        count[1] += 1
        rows = part_rows(side, p)
        copy = pltpu.make_async_copy(gath.at[rows, :], out_ref.at[rows, :], local_sem.at[at])
        copy.start()
        return copy

    barrier = pltpu.get_barrier_semaphore()
    for device in [other] + partner:
        pl.semaphore_signal(barrier, inc=1, device_id=device, device_id_type=pl.DeviceIdType.MESH)
    pl.semaphore_wait(barrier, 1 + n_bits)
    w_copy = pltpu.make_async_copy(w_hbm, w_ref, local_sem.at[2 * parts])
    w_copy.start()

    core = []
    for p in range(parts):
        product = dot(attn_ref[part_rows(1 - seg, p), :], grad_ref[...], ((1,), (0,)))
        core_out[p] = product.astype(jnp.bfloat16)
        core.append(send(core_out.at[p], core_in.at[p], other))
    places = [(p * size, 0) for p in range(parts)]
    history = [[] for _ in range(parts)]
    flying = [None] * parts
    for stage in range(n_bits):
        for p in range(parts):
            if stage == 0:
                acc[p * size : (p + 1) * size, :] = dot(
                    attn_ref[part_rows(seg, p), :], grad_ref[...], ((1,), (0,))
                )
                core[p].wait()
                arrived, at, shape = core_in.at[p], places[p], (size, acc.shape[1])
            else:
                flying[p].wait()
                arrived, (_, at, shape) = recvs[p][stage - 1], history[p][-1]
            add_arrived(acc, arrived, at, shape)
            b, dim = plans[p][stage]
            shape = sends[p][stage].shape
            keep, give = [
                tuple(at[d] + (which * shape[d] if d == dim else 0) for d in range(2))
                for which in (bit[b], 1 - bit[b])
            ]
            cast_given(acc, sends[p][stage], give, shape)
            flying[p] = send(sends[p][stage], recvs[p][stage], partner[b])
            history[p].append((b, keep, shape))
            if stage > 0:
                work()
        if stage == 0:
            w_copy.wait()
            for piece in chunks:
                piece()

    def gather(p, stage):
        b, keep, shape = history[p][stage]
        mine = region(gath, (seg * half + keep[0], keep[1]), shape)
        return send(mine, mine, partner[b])

    squares = jnp.zeros((1, 1), jnp.float32)
    for p in range(parts):
        flying[p].wait()
        _, keep, shape = history[p][-1]
        own = region(acc, keep, shape)[...] + recvs[p][-1][...].astype(jnp.float32)
        squares = squares + jnp.sum(own * own, keepdims=True)
        region(gath, (seg * half + keep[0], keep[1]), shape)[...] = own.astype(jnp.bfloat16)
        flying[p] = gather(p, n_bits - 1)
        work()
    square_out[0] = jnp.broadcast_to(squares, square_out.shape[1:])
    square_copy = send(square_out.at[0], square_in.at[0], partner[0])

    stores = []
    for stage in reversed(range(n_bits)):
        for p in range(parts):
            flying[p].wait()
            if stage > 0:
                flying[p] = gather(p, stage - 1)
            else:
                mine = gath.at[part_rows(seg, p), :]
                flying[p] = send(mine, mine, other)
                stores.append(store(seg, p))
            work()
        step = n_bits - 1 - stage
        square_copy.wait()
        square_out[step + 1] = square_out[step] + square_in[step]
        device = partner[step + 1] if step + 1 < n_bits else other
        square_copy = send(square_out.at[step + 1], square_in.at[step + 1], device)
    for head in heads:
        head()
    dq_ref[...] = dq_t[...].T.astype(jnp.bfloat16)
    square_copy.wait()
    square_ref[...] = square_out[n_bits] + square_in[n_bits]
    for p in range(parts):
        flying[p].wait()
        stores.append(store(1 - seg, p))
    for copy in stores:
        copy.wait()


def add_arrived(acc, arrived, at, shape):
    lanes = pl.ds(pl.multiple_of(at[1], 128), shape[1])

    def add(row, block):
        rows = pl.ds(pl.multiple_of(at[0] + row, BLOCK), block)
        acc[rows, lanes] += arrived[pl.ds(row, block), :].astype(jnp.float32)

    by_rows(shape[0], add)


def cast_given(acc, target, at, shape):
    lanes = pl.ds(pl.multiple_of(at[1], 128), shape[1])

    def cast(row, block):
        rows = pl.ds(pl.multiple_of(at[0] + row, BLOCK), block)
        target[pl.ds(row, block), :] = acc[rows, lanes].astype(jnp.bfloat16)

    by_rows(shape[0], cast)


def sum_weight(sums, head_size, plans, attn_t, out_grad, w_out, operands, grads):
    width, cols = attn_t.shape[0], out_grad.shape[1]
    half, bits, parts = width // 2, len(plans[0]), len(plans)
    low = functools.partial(pltpu.VMEM, dtype=jnp.bfloat16)
    shapes = [stage_shapes((half // parts, cols), plan) for plan in plans]
    buffers = [low(shape) for part in shapes for shape in part]
    copies = 2 * parts + 2 * parts * bits + bits + 1
    vmem = pl.BlockSpec(memory_space=pltpu.VMEM)
    hbm = pl.BlockSpec(memory_space=pl.ANY)
    tokens = out_grad.shape[0]
    total, squares, *results = pl.pallas_call(
        functools.partial(sum_kernel, plans, sums, head_size),
        in_specs=[vmem] * 2 + [hbm] + [vmem] * len(operands),
        out_specs=[hbm, vmem] + [vmem] * len(grads),
        out_shape=[
            jax.ShapeDtypeStruct((width, cols), jnp.bfloat16),
            jax.ShapeDtypeStruct((8, 128), jnp.float32),
            *grads,
        ],
        scratch_shapes=[
            pltpu.VMEM((half, cols), jnp.float32),
            low((parts, half // parts, cols)),
            low((parts, half // parts, cols)),
            low((width, cols)),
            pltpu.VMEM((bits + 1, 8, 128), jnp.float32),
            pltpu.VMEM((bits + 1, 8, 128), jnp.float32),
            low((width, cols)),
            low((tokens, width)),
            pltpu.VMEM((width, tokens), jnp.float32),
            *buffers,
            *buffers,
            pltpu.SemaphoreType.DMA((copies,)),
            pltpu.SemaphoreType.DMA((copies,)),
            pltpu.SemaphoreType.DMA((2 * parts + 1,)),
        ],
        compiler_params=pltpu.CompilerParams(
            collective_id=0, has_side_effects=True, vmem_limit_bytes=60 * 1024 * 1024
        ),
        cost_estimate=pl.CostEstimate(
            flops=2 * width * cols * attn_t.shape[1],
            bytes_accessed=4 * width * cols,
            transcendentals=0,
        ),
    )(attn_t, out_grad, w_out, *operands)
    rms = jnp.sqrt(squares[0, 0] / (width * cols) + 1e-06)
    low_grad = (total.astype(jnp.float32) * jnp.minimum(1.0, 1.0 / rms)).astype(jnp.bfloat16)
    return (*results, low_grad)


def solution(mesh):
    row = P("dp", "seg", None)
    return jax.shard_map(
        functools.partial(shards, mesh.shape["seg"], mesh.shape["dp"]),
        mesh=mesh,
        in_specs=(row,) * 6 + (P(),),
        out_specs=(row,) * 5 + (P(),),
        check_vma=False,
    )
```
